32 devices in a mesh: groups: 2 (over y), tm: 4 (over z), tile: 2 (over x), arrow: 2 (over core).
Axes of the slice: x: 2, y: 2, z: 4, core: 2. Of those that a mesh axis runs over, the one named last changes fastest.
Arguments:
- forward_blocks: float32 [8, 96, 1024], P(('groups', 'tm'), ('tile', 'arrow')), parts along dimension 0, may hold values from -3 to 3
- arrow_rhs: float32 [192, 64], P(('groups', 'tile', 'arrow')), parts along dimension 0, may hold values from -6 to 6
- diag_inverse: bfloat16 [8, 1024, 1024], P(('groups', 'tm'), None, ('tile', 'arrow')), parts along dimension 0
- lower_coupling: bfloat16 [8, 1024, 1024], P(('groups', 'tm'), None, ('tile', 'arrow')), parts along dimension 0
- arrow_slab: bfloat16 [8, 64, 1024], P(('groups', 'tm'), 'arrow'), parts along dimension 0, may hold values from -0.09375 to 0.09375
- arrow_inverse: float32 [128, 64], P('groups'), parts along dimension 0
- boundary_term: float32 [192, 1024], P(('groups', 'tile', 'arrow')), parts along dimension 0, may hold values from -6 to 6
Outputs:
- solution: float32 [8, 96, 1024], P(('groups', 'tm'), ('tile', 'arrow')), parts along dimension 0
- arrow_solution: float32 [192, 64], P(('groups', 'tile', 'arrow')), parts along dimension 0
The draws below stay inside these ranges and needn't reach their ends.
There are 2 independent parts, one for each index of `groups`. The reference program is written for one: setup_inputs(seed, part) draws one part's arguments, and reference() takes and returns one part's arrays. A program takes and returns all parts, laid end to end along the dimension named above; each array names one. Nothing has to cross between parts.
All inputs are finite; a program needn't handle non-finite values.
Results may differ from the reference program's by a relative error of at most 0.007.
Values may be sent and summed in bfloat16 or wider, within the bound.
A program may use at most 64 MiB of HBM per device.

```python
import math
import jax
import jax.numpy as jnp
from jax import lax

B = 1024
A = 64
TIME_BLOCKS = 4
R = 96


def coupled_factors(key):
    diag_key = jax.random.fold_in(key, 11)
    rate_key = jax.random.fold_in(key, 12)
    rough_key = jax.random.fold_in(key, 13)
    spike_key = jax.random.fold_in(key, 14)
    lower_key = jax.random.fold_in(key, 15)
    coupling_key = jax.random.fold_in(key, 16)
    diagonal = jnp.exp(jax.random.uniform(diag_key, (TIME_BLOCKS, B), jnp.float32, math.log(0.7), math.log(1.4)))
    baseline_rate = jax.random.uniform(rate_key, (B,), jnp.float32, 0.3, 0.99)
    roughness_factor = jax.random.uniform(rough_key, (TIME_BLOCKS, B), jnp.float32, 0.93, 1.0)
    spike_blocks = jax.random.randint(spike_key, (2,), 0, TIME_BLOCKS)
    block_position_index = jnp.arange(TIME_BLOCKS)
    inside_spike = jnp.any(block_position_index[:, None] == spike_blocks[None, :], axis=1)
    spike_factor = jnp.where(inside_spike, 0.7, 1.0).astype(jnp.float32)
    falloff_rate = baseline_rate[None, :] * roughness_factor * spike_factor[:, None]
    identity = jnp.eye(B, dtype=jnp.float32)
    strict_lower = jnp.tril(jnp.ones((B, B), jnp.float32), -1)
    lower_part = jax.random.normal(lower_key, (TIME_BLOCKS, B, B), jnp.float32) * (0.3 / math.sqrt(B))
    inverse = lower_part * strict_lower[None] + diagonal[:, :, None] * identity[None]
    coupling_part = jax.random.normal(coupling_key, (TIME_BLOCKS, B, B), jnp.float32) * (0.15 / math.sqrt(B))
    coupling = coupling_part * (1.0 - identity)[None] - (falloff_rate / diagonal)[:, :, None] * identity[None]
    return (inverse, coupling)


def draw_diag_inverse(key, part):
    return coupled_factors(key)[0].astype(jnp.bfloat16)


def draw_lower_coupling(key, part):
    return coupled_factors(key)[1].astype(jnp.bfloat16)


def draw_arrow_inverse(key, part):
    diag_key = jax.random.fold_in(key, 21)
    lower_key = jax.random.fold_in(key, 22)
    diagonal = jnp.exp(jax.random.uniform(diag_key, (A,), jnp.float32, math.log(0.7), math.log(1.4)))
    identity = jnp.eye(A, dtype=jnp.float32)
    strict_lower = jnp.tril(jnp.ones((A, A), jnp.float32), -1)
    lower_part = jax.random.normal(lower_key, (A, A), jnp.float32) * (0.3 / math.sqrt(A))
    return lower_part * strict_lower + diagonal[:, None] * identity


def steps_of(rng, dims, pieces, smallest, largest):
    gain = 1.0
    for axis_at, blocks in pieces:
        heights = jax.random.uniform(jax.random.fold_in(jax.random.fold_in(rng, 6), axis_at), (blocks,), jnp.float32, smallest / len(pieces), largest / len(pieces))
        gain = gain * jnp.repeat(jnp.exp(heights), dims[axis_at] // blocks).reshape((-1,) + (1,) * (len(dims) - 1 - axis_at))
    return gain


def centred(own_key, extent, spread, reach, split=(), kind=jnp.bfloat16):
    values = spread * jax.random.normal(own_key, extent, jnp.float32)
    if split:
        values = values * steps_of(own_key, extent, split, -0.22, 0.18)
    return jnp.clip(values, -reach, reach).astype(kind)


def setup_inputs(seed: int = 0, part: int = 0) -> dict:
    key_of = jax.random.split(jax.random.key(seed), 8)
    part_keys = jax.random.split(jax.random.fold_in(key_of[7], part), 8)
    return {
        "forward_blocks": centred(part_keys[0], (TIME_BLOCKS, R, B), 0.5, 3.0, ((0, 4), (1, 4)), jnp.float32),
        "arrow_rhs": centred(part_keys[1], (R, A), 1.0, 6.0, ((0, 4),), jnp.float32),
        "diag_inverse": draw_diag_inverse(jax.random.fold_in(jax.random.fold_in(key_of[7], part), 71), part),
        "lower_coupling": draw_lower_coupling(jax.random.fold_in(jax.random.fold_in(key_of[7], part), 71), part),
        "arrow_slab": centred(part_keys[4], (TIME_BLOCKS, A, B), (4 * B) ** -0.5, 0.09375, ((0, 4), (1, 2))),
        "arrow_inverse": draw_arrow_inverse(jax.random.fold_in(jax.random.fold_in(key_of[7], part), 71), part),
        "boundary_term": centred(part_keys[6], (R, B), 1.0, 6.0, ((0, 4),), jnp.float32),
    }


def reference(forward_blocks, arrow_rhs, diag_inverse, lower_coupling, arrow_slab, arrow_inverse, boundary_term):
    highest = lax.Precision.HIGHEST
    slab_wide = arrow_slab.astype(jnp.float32)
    arrow_sum = jnp.einsum("trb,tab->ra", forward_blocks, slab_wide, precision=highest)
    arrow_forward = jnp.dot(arrow_rhs - arrow_sum, arrow_inverse.T, precision=highest)
    arrow_solution = jnp.dot(arrow_forward, arrow_inverse, precision=highest)
    arrow_term = jnp.einsum("ra,tab->trb", arrow_solution, slab_wide, precision=highest)
    source_rows = forward_blocks - arrow_term

    def backward(carry_in, block_items):
        source_block, inverse_block, lower_block = block_items
        coupling = jnp.dot(inverse_block, lower_block, preferred_element_type=jnp.float32).astype(jnp.bfloat16)
        residual = source_block - carry_in
        rounded = residual.astype(jnp.bfloat16)
        solution = jnp.dot(rounded, inverse_block, preferred_element_type=jnp.float32)
        carry_out = jnp.dot(residual, coupling.astype(jnp.float32), precision=highest)
        return carry_out, solution

    final_carry, solution = lax.scan(backward, boundary_term, (source_rows, diag_inverse, lower_coupling), reverse=True)
    return solution, arrow_solution
```

```python
import functools

import jax
import jax.numpy as jnp
from jax import lax
from jax.experimental import pallas as pl
from jax.experimental.pallas import tpu as pltpu
from jax.sharding import PartitionSpec as P

MESH = pl.DeviceIdType.MESH
BF16 = jnp.bfloat16
F32 = jnp.float32
UNROLL_LIMIT = 8


def for_each(first, last, body):
    if last - first <= UNROLL_LIMIT:
        for i in range(first, last):
            body(i)
    else:
        pl.loop(first, last)(body)


def dot(a, b, **kwargs):
    return jnp.dot(a, b, preferred_element_type=F32, **kwargs)


def kernel(
    nt,
    nh,
    fwd_hbm,
    rhs_hbm,
    diag_hbm,
    lower_hbm,
    slab_hbm,
    inv_hbm,
    bound_hbm,
    sol_hbm,
    arrow_hbm,
    fwd,
    rhs,
    inv,
    bound,
    slab,
    diag,
    lower,
    source,
    parts,
    resid,
    accum,
    outgoing,
    incoming,
    finished,
    arrow_out,
    local_sem,
    slab_sem,
    diag_sem,
    source_sems,
    lower_sems,
    relay_sems,
    parts_sems,
    chain_sems,
    out_sems,
):
    t = lax.axis_index("tm")
    h = lax.axis_index("tile")
    core = lax.axis_index("arrow")
    sibling = {"arrow": 1 - core}
    rows = fwd.shape[0]
    width = diag.shape[2]
    wide = 2 * width
    chunks = 2 * nh
    halves = slab.shape[0] // 2
    fixed = slab.shape[0]
    me = t * nh + h
    own_rows = pl.ds(pl.multiple_of(core * halves, halves), halves)

    def tile_rows(j):
        return pl.ds(pl.multiple_of(j * wide, wide), wide)

    def remote(src, dst, send, recv, device):
        return pltpu.make_async_remote_copy(
            src_ref=src,
            dst_ref=dst,
            send_sem=send,
            recv_sem=recv,
            device_id=device,
            device_id_type=MESH,
        )

    def local(src, dst, index):
        return pltpu.make_async_copy(src, dst, local_sem.at[index])

    loads = [
        local(fwd_hbm.at[0], fwd, 0),
        local(slab_hbm.at[0], slab.at[own_rows], 1),
        local(bound_hbm, bound, 2),
        local(rhs_hbm, rhs, 3),
        local(inv_hbm, inv, 4),
        local(diag_hbm.at[0], diag.at[core], 5),
        local(lower_hbm.at[0, tile_rows(h)], lower.at[2 * h + core], 6),
    ]
    for load in loads:
        load.start()

    def coords(index):
        return {"tm": index // nh, "tile": lax.rem(index, nh)}

    def partner(k):
        return lax.rem(me + k, nt * nh)

    def across(k):
        return lax.rem(h + k, nh)

    barrier = pltpu.get_barrier_semaphore()
    pl.semaphore_signal(barrier, inc=1, device_id=sibling, device_id_type=MESH)

    def greet(k):
        pl.semaphore_signal(barrier, inc=1, device_id=coords(partner(k)), device_id_type=MESH)

    for_each(1, nt * nh, greet)
    pl.semaphore_wait(barrier, nt * nh)

    send_slab = remote(
        slab_hbm.at[0], slab.at[own_rows], slab_sem.at[0], slab_sem.at[1], sibling
    )
    send_slab.start()

    loads[0].wait()
    loads[2].wait()
    is_last = (t == nt - 1).astype(F32)
    source[h] = fwd[...] - is_last * bound[...]
    sends = []
    for k in range(1, nh):
        j = across(k)
        copy = remote(
            source.at[h], source.at[h], source_sems.at[0, j], source_sems.at[1, h], {"tile": j}
        )
        copy.start()
        sends.append(copy)
    for k in range(1, nh):
        j = across(k)
        slot = 2 * h + core
        copy = remote(
            lower_hbm.at[0, tile_rows(j)],
            lower.at[slot],
            lower_sems.at[0, j],
            lower_sems.at[1, h],
            {"tile": j},
        )
        copy.start()
        sends.append(copy)
    send_diag = remote(diag_hbm.at[0], diag.at[core], diag_sem.at[0], diag_sem.at[1], sibling)
    send_diag.start()
    relays = [
        remote(
            lower_hbm.at[0, tile_rows(h)],
            lower.at[2 * h + core],
            relay_sems.at[0, h],
            relay_sems.at[1, h],
            sibling,
        )
    ]
    relays[0].start()

    high = fwd[...].astype(BF16)
    low = (fwd[...] - high.astype(F32)).astype(BF16)
    loads[1].wait()
    send_slab.wait()
    contract = (((1,), (1,)), ((), ()))
    part = lax.dot_general(high, slab[...], contract, preferred_element_type=F32)
    part = part + lax.dot_general(low, slab[...], contract, preferred_element_type=F32)
    loads[3].wait()
    parts[me] = (t == 0).astype(F32) * rhs[...] - part

    def part_copy(k):
        other = partner(k)
        return remote(
            parts.at[me], parts.at[me], parts_sems.at[0, other], parts_sems.at[1, me], coords(other)
        )

    for_each(1, nt * nh, lambda k: part_copy(k).start())

    highest = lax.Precision.HIGHEST
    loads[4].wait()
    gram = lax.dot_general(
        inv[...], inv[...], (((0,), (0,)), ((), ())), precision=highest, preferred_element_type=F32
    )

    def part_arrived(k):
        other = partner(k)
        remote(
            parts.at[other],
            parts.at[other],
            parts_sems.at[0, other],
            parts_sems.at[1, other],
            coords(other),
        ).wait_recv()

    for_each(1, nt * nh, part_arrived)
    total = parts[0:nh]
    for i in range(1, nt):
        total = total + parts[i * nh : (i + 1) * nh]
    answer = dot(total.reshape(nh * rows, fixed), gram, precision=highest)
    arrow_out[...] = answer.reshape(nh, rows, fixed)
    write_arrow = pltpu.make_async_copy(arrow_out.at[h], arrow_hbm, local_sem.at[7])
    write_arrow.start()
    answer = answer.astype(BF16)

    for k in range(1, nh):
        j = across(k)
        remote(
            source.at[j], source.at[j], source_sems.at[0, j], source_sems.at[1, j], {"tile": j}
        ).wait_recv()
    for c in range(chunks):
        columns = slice(c * width, (c + 1) * width)
        resid[c] = source[:, :, columns].reshape(nh * rows, width) - dot(answer, slab[:, columns])

    for k in range(1, nh):
        j = across(k)
        slot = lower.at[2 * j + core]
        remote(slot, slot, lower_sems.at[0, j], lower_sems.at[1, j], {"tile": j}).wait_recv()
        copy = remote(slot, slot, relay_sems.at[0, j], relay_sems.at[1, j], sibling)
        copy.start()
        relays.append(copy)

    def lower_arrived():
        loads[6].wait()
        for k in range(nh):
            j = across(k)
            slot = lower.at[2 * j + 1 - core]
            remote(slot, slot, relay_sems.at[0, j], relay_sems.at[1, j], sibling).wait_recv()

    loads[5].wait()
    other_diag = diag.at[1 - core]
    remote(other_diag, other_diag, diag_sem.at[0], diag_sem.at[1], sibling).wait_recv()

    pl.when(t < nt - 1)(lower_arrived)

    accum[...] = jnp.zeros_like(accum)
    for c in reversed(range(chunks)):

        @pl.when(2 * h <= c)
        def _():
            @pl.when(t < nt - 1)
            def _():
                carry = None
                for j in range(nh):
                    slot = incoming.at[j, c]
                    remote(
                        slot,
                        slot,
                        chain_sems.at[0, j, c],
                        chain_sems.at[1, j, c],
                        {"tm": lax.rem(t + 1, nt)},
                    ).wait_recv()
                    term = incoming[j, c].astype(F32)
                    carry = term if carry is None else carry + term
                resid[c] = resid[c] - carry

            rounded = resid[c].astype(BF16)
            for b in range(2):
                accum[b] += dot(rounded, diag[b, c * width : (c + 1) * width, :])

    pl.when(t == nt - 1)(lower_arrived)

    def chain_copy(c, j):
        return remote(
            outgoing.at[c],
            incoming.at[h, c],
            chain_sems.at[0, j, c],
            chain_sems.at[1, h, c],
            {"tm": lax.rem(t + nt - 1, nt), "tile": j},
        )

    @pl.when(t > 0)
    def _():
        first, second = accum[0].astype(BF16), accum[1].astype(BF16)
        for c in reversed(range(chunks)):
            product = dot(first, lower[c, 0:width, :]) + dot(second, lower[c, width:wide, :])
            outgoing[c] = product.astype(BF16)
            for j in range(nh):
                if 2 * j <= c:
                    chain_copy(c, j).start()

    for b in range(2):
        finished[:, :, b * width : (b + 1) * width] = accum[b].reshape(nh, rows, width)
    for k in range(1, nh):
        j = across(k)
        copy = remote(
            finished.at[j],
            sol_hbm.at[0, :, tile_rows(h)],
            out_sems.at[0, j],
            out_sems.at[1, h],
            {"tile": j},
        )
        copy.start()
        sends.append(copy)
    write_own = pltpu.make_async_copy(
        finished.at[h], sol_hbm.at[0, :, tile_rows(h)], local_sem.at[8]
    )
    write_own.start()

    for_each(1, nt * nh, lambda k: part_copy(k).wait_send())
    send_diag.wait_send()
    for copy in sends + relays:
        copy.wait_send()

    @pl.when(t > 0)
    def _():
        for c in range(chunks):
            for j in range(nh):
                if 2 * j <= c:
                    chain_copy(c, j).wait_send()

    write_arrow.wait()
    write_own.wait()
    for k in range(1, nh):
        j = across(k)
        slot = sol_hbm.at[0, :, tile_rows(j)]
        remote(slot, slot, out_sems.at[0, j], out_sems.at[1, j], {"tile": j}).wait_recv()


def solution(mesh):
    nt, nh = mesh.shape["tm"], mesh.shape["tile"]

    def shards(forward, rhs, diag, lower, slab, inverse, boundary):
        _, rows, size = forward.shape
        width = diag.shape[2]
        fixed = rhs.shape[1]
        chunks = 2 * nh
        everything = pl.BlockSpec(memory_space=pl.ANY)
        dma = pltpu.SemaphoreType.DMA
        return pl.pallas_call(
            functools.partial(kernel, nt, nh),
            out_shape=(
                jax.ShapeDtypeStruct(forward.shape, F32),
                jax.ShapeDtypeStruct(rhs.shape, F32),
            ),
            in_specs=[everything] * 7,
            out_specs=(everything, everything),
            scratch_shapes=[
                pltpu.VMEM((rows, size), F32),
                pltpu.VMEM((rows, fixed), F32),
                pltpu.VMEM((fixed, fixed), F32),
                pltpu.VMEM((rows, size), F32),
                pltpu.VMEM((fixed, size), BF16),
                pltpu.VMEM((2, size, width), BF16),
                pltpu.VMEM((chunks, 2 * width, width), BF16),
                pltpu.VMEM((nh, rows, size), F32),
                pltpu.VMEM((nt * nh, rows, fixed), F32),
                pltpu.VMEM((chunks, nh * rows, width), F32),
                pltpu.VMEM((2, nh * rows, width), F32),
                pltpu.VMEM((chunks, nh * rows, width), BF16),
                pltpu.VMEM((nh, chunks, nh * rows, width), BF16),
                pltpu.VMEM((nh, rows, 2 * width), F32),
                pltpu.VMEM((nh, rows, fixed), F32),
                dma((9,)),
                dma((2,)),
                dma((2,)),
                dma((2, nh)),
                dma((2, nh)),
                dma((2, nh)),
                dma((2, nt * nh)),
                dma((2, nh, chunks)),
                dma((2, nh)),
            ],
            compiler_params=pltpu.CompilerParams(
                collective_id=0, has_side_effects=True, vmem_limit_bytes=32 * 1024 * 1024
            ),
        )(forward, rhs, diag, lower, slab, inverse, boundary)

    return jax.shard_map(
        shards,
        mesh=mesh,
        in_specs=(
            P(("groups", "tm"), ("tile", "arrow"), None),
            P(("groups", "tile", "arrow"), None),
            P(("groups", "tm"), None, ("tile", "arrow")),
            P(("groups", "tm"), None, ("tile", "arrow")),
            P(("groups", "tm"), "arrow", None),
            P("groups", None),
            P(("groups", "tile", "arrow"), None),
        ),
        out_specs=(
            P(("groups", "tm"), ("tile", "arrow"), None),
            P(("groups", "tile", "arrow"), None),
        ),
        check_vma=False,
    )
```

```python
import functools

import jax
import jax.numpy as jnp
from jax import lax
from jax.experimental import pallas as pl
from jax.experimental.pallas import tpu as pltpu
from jax.sharding import PartitionSpec as P

MESH = pl.DeviceIdType.MESH
BF16 = jnp.bfloat16
F32 = jnp.float32
UNROLL_LIMIT = 8


def for_each(first, last, body):
    if last - first <= UNROLL_LIMIT:
        for i in range(first, last):
            body(i)
    else:
        pl.loop(first, last)(body)


def dot(a, b, **kwargs):
    return jnp.dot(a, b, preferred_element_type=F32, **kwargs)


def kernel(
    nt,
    nh,
    fwd_hbm,
    rhs_hbm,
    diag_hbm,
    lower_hbm,
    slab_hbm,
    inv_hbm,
    bound_hbm,
    sol_hbm,
    arrow_hbm,
    fwd,
    rhs,
    inv,
    bound,
    slab,
    diag,
    lower,
    source,
    parts,
    resid,
    accum,
    outgoing,
    incoming,
    row_outgoing,
    row_incoming,
    row_accum,
    finished,
    arrow_out,
    local_sem,
    slab_sem,
    diag_sem,
    source_sems,
    lower_sems,
    relay_sems,
    parts_sems,
    chain_sems,
    out_sems,
    row_sems,
):
    t = lax.axis_index("tm")
    h = lax.axis_index("tile")
    core = lax.axis_index("arrow")
    sibling = {"arrow": 1 - core}
    rows = fwd.shape[0]
    width = diag.shape[2]
    wide = 2 * width
    chunks = 2 * nh
    halves = slab.shape[0] // 2
    fixed = slab.shape[0]
    me = t * nh + h
    own_rows = pl.ds(pl.multiple_of(core * halves, halves), halves)

    def tile_rows(j):
        return pl.ds(pl.multiple_of(j * wide, wide), wide)

    def remote(src, dst, send, recv, device):
        return pltpu.make_async_remote_copy(
            src_ref=src,
            dst_ref=dst,
            send_sem=send,
            recv_sem=recv,
            device_id=device,
            device_id_type=MESH,
        )

    def local(src, dst, index):
        return pltpu.make_async_copy(src, dst, local_sem.at[index])

    loads = [
        local(fwd_hbm.at[0], fwd, 0),
        local(slab_hbm.at[0], slab.at[own_rows], 1),
        local(bound_hbm, bound, 2),
        local(rhs_hbm, rhs, 3),
        local(inv_hbm, inv, 4),
        local(diag_hbm.at[0], diag.at[2 * h + core], 5),
    ]
    for load in loads:
        load.start()
    load_lower = local(lower_hbm.at[0, tile_rows(h)], lower.at[2 * h + core], 6)
    pl.when(t > 0)(load_lower.start)

    def coords(index):
        return {"tm": index // nh, "tile": lax.rem(index, nh)}

    def partner(k):
        return lax.rem(me + k, nt * nh)

    def across(k):
        return lax.rem(h + k, nh)

    barrier = pltpu.get_barrier_semaphore()
    pl.semaphore_signal(barrier, inc=1, device_id=sibling, device_id_type=MESH)

    def greet(k):
        pl.semaphore_signal(barrier, inc=1, device_id=coords(partner(k)), device_id_type=MESH)

    for_each(1, nt * nh, greet)
    pl.semaphore_wait(barrier, nt * nh)

    send_slab = remote(
        slab_hbm.at[0], slab.at[own_rows], slab_sem.at[0], slab_sem.at[1], sibling
    )
    send_slab.start()

    loads[0].wait()
    loads[2].wait()
    is_last = (t == nt - 1).astype(F32)
    source[h] = fwd[...] - is_last * bound[...]
    mine = 2 * h + core

    def source_copy(j):
        return remote(
            source.at[h], source.at[h], source_sems.at[0, j], source_sems.at[1, h], {"tile": j}
        )

    def lower_copy(j):
        return remote(
            lower_hbm.at[0, tile_rows(j)],
            lower.at[mine],
            lower_sems.at[0, j],
            lower_sems.at[1, h],
            {"tile": j},
        )

    def diag_copy(j):
        return remote(
            diag_hbm.at[0], diag.at[mine], lower_sems.at[0, j], lower_sems.at[1, h], {"tile": j}
        )

    own_relay = remote(
        lower_hbm.at[0, tile_rows(h)],
        lower.at[mine],
        relay_sems.at[0, h],
        relay_sems.at[1, h],
        sibling,
    )

    @pl.when(t > 0)
    def _():
        for k in range(1, nh):
            source_copy(across(k)).start()
        for k in range(1, nh):
            lower_copy(across(k)).start()
        own_relay.start()

    @pl.when(t == 0)
    def _():
        for k in range(1, nh):
            diag_copy(across(k)).start()

    send_diag = remote(diag_hbm.at[0], diag.at[mine], diag_sem.at[0], diag_sem.at[1], sibling)
    send_diag.start()

    high = fwd[...].astype(BF16)
    low = (fwd[...] - high.astype(F32)).astype(BF16)
    loads[1].wait()
    send_slab.wait()
    contract = (((1,), (1,)), ((), ()))
    part = lax.dot_general(high, slab[...], contract, preferred_element_type=F32)
    part = part + lax.dot_general(low, slab[...], contract, preferred_element_type=F32)
    loads[3].wait()
    parts[me] = (t == 0).astype(F32) * rhs[...] - part

    def part_copy(k):
        other = partner(k)
        return remote(
            parts.at[me], parts.at[me], parts_sems.at[0, other], parts_sems.at[1, me], coords(other)
        )

    for_each(1, nt * nh, lambda k: part_copy(k).start())

    highest = lax.Precision.HIGHEST
    loads[4].wait()
    gram = lax.dot_general(
        inv[...], inv[...], (((0,), (0,)), ((), ())), precision=highest, preferred_element_type=F32
    )

    def part_arrived(k):
        other = partner(k)
        remote(
            parts.at[other],
            parts.at[other],
            parts_sems.at[0, other],
            parts_sems.at[1, other],
            coords(other),
        ).wait_recv()

    for_each(1, nt * nh, part_arrived)
    total = parts[0:nh]
    for i in range(1, nt):
        total = total + parts[i * nh : (i + 1) * nh]
    answer = dot(total.reshape(nh * rows, fixed), gram, precision=highest)
    arrow_out[...] = answer.reshape(nh, rows, fixed)
    write_arrow = pltpu.make_async_copy(arrow_out.at[h], arrow_hbm, local_sem.at[8])
    write_arrow.start()
    answer = answer.astype(BF16)

    def relay(array, j):
        slot = array.at[2 * j + core]
        return remote(slot, slot, relay_sems.at[0, j], relay_sems.at[1, j], sibling)

    def relay_all(array):
        for k in range(1, nh):
            j = across(k)
            slot = array.at[2 * j + core]
            remote(slot, slot, lower_sems.at[0, j], lower_sems.at[1, j], {"tile": j}).wait_recv()
            relay(array, j).start()

    def relayed(array, first):
        for k in range(first, nh):
            j = across(k)
            slot = array.at[2 * j + 1 - core]
            remote(slot, slot, relay_sems.at[0, j], relay_sems.at[1, j], sibling).wait_recv()

    def diag_arrived():
        loads[5].wait()
        slot = diag.at[2 * h + 1 - core]
        remote(slot, slot, diag_sem.at[0], diag_sem.at[1], sibling).wait_recv()

    def lower_arrived():
        load_lower.wait()
        relayed(lower, 0)

    def chain_copy(c, j):
        return remote(
            outgoing.at[c],
            incoming.at[h, c],
            chain_sems.at[0, j, c],
            chain_sems.at[1, h, c],
            {"tm": lax.rem(t + nt - 1, nt), "tile": j},
        )

    def row_copy(q, j):
        return remote(
            row_outgoing.at[q, j],
            row_incoming.at[h, q],
            row_sems.at[0, j, q],
            row_sems.at[1, h, q],
            {"tm": lax.rem(t + nt - 1, nt), "tile": j},
        )

    def out_copy(j):
        return remote(
            finished.at[j],
            sol_hbm.at[0, :, tile_rows(h)],
            out_sems.at[0, j],
            out_sems.at[1, h],
            {"tile": j},
        )

    @pl.when(t > 0)
    def _():
        for k in range(1, nh):
            j = across(k)
            remote(
                source.at[j], source.at[j], source_sems.at[0, j], source_sems.at[1, j], {"tile": j}
            ).wait_recv()
        for c in range(chunks):
            columns = slice(c * width, (c + 1) * width)
            resid[c] = source[:, :, columns].reshape(nh * rows, width) - dot(
                answer, slab[:, columns]
            )
        accum[...] = jnp.zeros_like(accum)
        relay_all(lower)
        diag_arrived()
        pl.when(t < nt - 1)(lower_arrived)
        for c in reversed(range(chunks)):

            @pl.when(2 * h <= c)
            def _():
                @pl.when(t < nt - 1)
                def _():
                    carry = None
                    for j in range(nh):
                        slot = incoming.at[j, c]
                        remote(
                            slot,
                            slot,
                            chain_sems.at[0, j, c],
                            chain_sems.at[1, j, c],
                            {"tm": lax.rem(t + 1, nt)},
                        ).wait_recv()
                        term = incoming[j, c].astype(F32)
                        carry = term if carry is None else carry + term
                    resid[c] = resid[c] - carry

                rounded = resid[c].astype(BF16)
                for b in range(2):
                    accum[b] += dot(rounded, diag[2 * h + b, c * width : (c + 1) * width, :])

        pl.when(t == nt - 1)(lower_arrived)
        first, second = accum[0].astype(BF16), accum[1].astype(BF16)

        def product(c):
            return dot(first, lower[c, 0:width, :]) + dot(second, lower[c, width:wide, :])

        @pl.when(t > 1)
        def _():
            for c in reversed(range(chunks)):
                outgoing[c] = product(c).astype(BF16)
                for j in range(nh):
                    if 2 * j <= c:
                        chain_copy(c, j).start()

        @pl.when(t == 1)
        def _():
            for q in reversed(range(nh)):
                left, right = product(2 * q), product(2 * q + 1)
                for j in range(nh):
                    mix = slice(j * rows, (j + 1) * rows)
                    both = jnp.concatenate([left[mix], right[mix]], axis=0)
                    row_outgoing[q, j] = both.astype(BF16)
                    row_copy(q, j).start()

        for b in range(2):
            finished[:, :, b * width : (b + 1) * width] = accum[b].reshape(nh, rows, width)
        for k in range(1, nh):
            out_copy(across(k)).start()
        write_own = pltpu.make_async_copy(
            finished.at[h], sol_hbm.at[0, :, tile_rows(h)], local_sem.at[7]
        )
        write_own.start()

        for k in range(1, nh):
            j = across(k)
            source_copy(j).wait_send()
            lower_copy(j).wait_send()
            relay(lower, j).wait_send()
            out_copy(j).wait_send()
        own_relay.wait_send()

        @pl.when(t > 1)
        def _():
            for c in range(chunks):
                for j in range(nh):
                    if 2 * j <= c:
                        chain_copy(c, j).wait_send()

        @pl.when(t == 1)
        def _():
            for q in range(nh):
                for j in range(nh):
                    row_copy(q, j).wait_send()

        write_own.wait()
        for k in range(1, nh):
            j = across(k)
            slot = sol_hbm.at[0, :, tile_rows(j)]
            remote(slot, slot, out_sems.at[0, j], out_sems.at[1, j], {"tile": j}).wait_recv()

    @pl.when(t == 0)
    def _():
        own_answer = arrow_out[h].astype(BF16)
        for c in range(chunks):
            columns = slice(c * width, (c + 1) * width)
            resid[c, 0:rows, :] = source[h, :, columns] - dot(own_answer, slab[:, columns])
        row_accum[...] = jnp.zeros_like(row_accum)
        relay_all(diag)
        diag_arrived()
        relayed(diag, 1)
        for q in reversed(range(nh)):
            if nt > 1:
                carry = None
                for j in range(nh):
                    slot = row_incoming.at[j, q]
                    remote(
                        slot,
                        slot,
                        row_sems.at[0, j, q],
                        row_sems.at[1, j, q],
                        {"tm": lax.rem(t + 1, nt)},
                    ).wait_recv()
                    term = row_incoming[j, q].astype(F32)
                    carry = term if carry is None else carry + term
            for c in (2 * q + 1, 2 * q):
                value = resid[c, 0:rows, :]
                if nt > 1:
                    at = (c - 2 * q) * rows
                    value = value - carry[at : at + rows]
                rounded = value.astype(BF16)
                for b in range(c + 1):
                    row_accum[:, b * width : (b + 1) * width] += dot(
                        rounded, diag[b, c * width : (c + 1) * width, :]
                    )
        write_rows = pltpu.make_async_copy(row_accum, sol_hbm.at[0], local_sem.at[7])
        write_rows.start()
        for k in range(1, nh):
            j = across(k)
            diag_copy(j).wait_send()
            relay(diag, j).wait_send()
        write_rows.wait()

    for_each(1, nt * nh, lambda k: part_copy(k).wait_send())
    send_diag.wait_send()
    write_arrow.wait()


def solution(mesh):
    nt, nh = mesh.shape["tm"], mesh.shape["tile"]

    def shards(forward, rhs, diag, lower, slab, inverse, boundary):
        _, rows, size = forward.shape
        width = diag.shape[2]
        fixed = rhs.shape[1]
        chunks = 2 * nh
        everything = pl.BlockSpec(memory_space=pl.ANY)
        dma = pltpu.SemaphoreType.DMA
        return pl.pallas_call(
            functools.partial(kernel, nt, nh),
            out_shape=(
                jax.ShapeDtypeStruct(forward.shape, F32),
                jax.ShapeDtypeStruct(rhs.shape, F32),
            ),
            in_specs=[everything] * 7,
            out_specs=(everything, everything),
            scratch_shapes=[
                pltpu.VMEM((rows, size), F32),
                pltpu.VMEM((rows, fixed), F32),
                pltpu.VMEM((fixed, fixed), F32),
                pltpu.VMEM((rows, size), F32),
                pltpu.VMEM((fixed, size), BF16),
                pltpu.VMEM((chunks, size, width), BF16),
                pltpu.VMEM((chunks, 2 * width, width), BF16),
                pltpu.VMEM((nh, rows, size), F32),
                pltpu.VMEM((nt * nh, rows, fixed), F32),
                pltpu.VMEM((chunks, nh * rows, width), F32),
                pltpu.VMEM((2, nh * rows, width), F32),
                pltpu.VMEM((chunks, nh * rows, width), BF16),
                pltpu.VMEM((nh, chunks, nh * rows, width), BF16),
                pltpu.VMEM((nh, nh, 2 * rows, width), BF16),
                pltpu.VMEM((nh, nh, 2 * rows, width), BF16),
                pltpu.VMEM((rows, size), F32),
                pltpu.VMEM((nh, rows, 2 * width), F32),
                pltpu.VMEM((nh, rows, fixed), F32),
                dma((9,)),
                dma((2,)),
                dma((2,)),
                dma((2, nh)),
                dma((2, nh)),
                dma((2, nh)),
                dma((2, nt * nh)),
                dma((2, nh, chunks)),
                dma((2, nh)),
                dma((2, nh, nh)),
            ],
            compiler_params=pltpu.CompilerParams(
                collective_id=0, has_side_effects=True, vmem_limit_bytes=60 * 1024 * 1024
            ),
        )(forward, rhs, diag, lower, slab, inverse, boundary)

    return jax.shard_map(
        shards,
        mesh=mesh,
        in_specs=(
            P(("groups", "tm"), ("tile", "arrow"), None),
            P(("groups", "tile", "arrow"), None),
            P(("groups", "tm"), None, ("tile", "arrow")),
            P(("groups", "tm"), None, ("tile", "arrow")),
            P(("groups", "tm"), "arrow", None),
            P("groups", None),
            P(("groups", "tile", "arrow"), None),
        ),
        out_specs=(
            P(("groups", "tm"), ("tile", "arrow"), None),
            P(("groups", "tile", "arrow"), None),
        ),
        check_vma=False,
    )
```

```python
import functools

import jax
import jax.numpy as jnp
from jax import lax
from jax.experimental import pallas as pl
from jax.experimental.pallas import tpu as pltpu
from jax.sharding import PartitionSpec as P

MESH = pl.DeviceIdType.MESH
BF16 = jnp.bfloat16
F32 = jnp.float32
UNROLL_LIMIT = 8


def for_each(first, last, body):
    if last - first <= UNROLL_LIMIT:
        for i in range(first, last):
            body(i)
    else:
        pl.loop(first, last)(body)


def dot(a, b, **kwargs):
    return jnp.dot(a, b, preferred_element_type=F32, **kwargs)


def kernel(
    nt,
    nh,
    fwd_hbm,
    rhs_hbm,
    diag_hbm,
    lower_hbm,
    slab_hbm,
    inv_hbm,
    bound_hbm,
    sol_hbm,
    arrow_hbm,
    fwd,
    rhs,
    inv,
    bound,
    slab,
    diag,
    lower,
    source,
    packed,
    parts,
    resid,
    accum,
    outgoing,
    incoming,
    row_outgoing,
    row_incoming,
    row_accum,
    finished,
    arrow_out,
    local_sem,
    slab_sem,
    diag_sem,
    source_sems,
    lower_sems,
    relay_sems,
    parts_sems,
    chain_sems,
    out_sems,
    row_sems,
):
    t = lax.axis_index("tm")
    h = lax.axis_index("tile")
    core = lax.axis_index("arrow")
    sibling = {"arrow": 1 - core}
    rows = fwd.shape[0]
    size = diag.shape[1]
    width = diag.shape[2]
    wide = 2 * width
    chunks = 2 * nh
    halves = slab.shape[0] // 2
    fixed = slab.shape[0]
    me = t * nh + h
    own_rows = pl.ds(pl.multiple_of(core * halves, halves), halves)

    def tile_rows(j):
        return pl.ds(pl.multiple_of(j * wide, wide), wide)

    def remote(src, dst, send, recv, device):
        return pltpu.make_async_remote_copy(
            src_ref=src,
            dst_ref=dst,
            send_sem=send,
            recv_sem=recv,
            device_id=device,
            device_id_type=MESH,
        )

    def local(src, dst, index):
        return pltpu.make_async_copy(src, dst, local_sem.at[index])

    loads = [
        local(fwd_hbm.at[0], fwd, 0),
        local(slab_hbm.at[0], slab.at[own_rows], 1),
        local(bound_hbm, bound, 2),
        local(rhs_hbm, rhs, 3),
        local(inv_hbm, inv, 4),
        local(diag_hbm.at[0], diag.at[2 * h + core], 5),
    ]
    for load in loads:
        load.start()
    load_lower = local(lower_hbm.at[0, tile_rows(h)], lower.at[2 * h + core], 6)
    pl.when(t > 0)(load_lower.start)

    def coords(index):
        return {"tm": index // nh, "tile": lax.rem(index, nh)}

    def partner(k):
        return lax.rem(me + k, nt * nh)

    def across(k):
        return lax.rem(h + k, nh)

    barrier = pltpu.get_barrier_semaphore()
    pl.semaphore_signal(barrier, inc=1, device_id=sibling, device_id_type=MESH)

    def greet(k):
        pl.semaphore_signal(barrier, inc=1, device_id=coords(partner(k)), device_id_type=MESH)

    for_each(1, nt * nh, greet)
    pl.semaphore_wait(barrier, nt * nh)

    send_slab = remote(
        slab_hbm.at[0], slab.at[own_rows], slab_sem.at[0], slab_sem.at[1], sibling
    )
    send_slab.start()

    is_last = (t == nt - 1).astype(F32)
    mine = 2 * h + core

    def source_copy(j):
        return remote(
            packed.at[h], packed.at[h], source_sems.at[0, j], source_sems.at[1, h], {"tile": j}
        )

    def piece_of(i):
        return slice(i * width, (i + 1) * width)

    def lower_copy(j, i):
        return remote(
            lower_hbm.at[0, pl.ds(pl.multiple_of(j * wide + i * width, width), width)],
            lower.at[mine, piece_of(i)],
            lower_sems.at[0, j, i],
            lower_sems.at[1, h, i],
            {"tile": j},
        )

    def diag_copy(j):
        return remote(
            diag_hbm.at[0],
            diag.at[mine],
            lower_sems.at[0, j, 0],
            lower_sems.at[1, h, 0],
            {"tile": j},
        )

    own_relay = remote(
        lower_hbm.at[0, tile_rows(h)],
        lower.at[mine],
        relay_sems.at[0, h, 0],
        relay_sems.at[1, h, 0],
        sibling,
    )

    @pl.when(t > 0)
    def _():
        for k in range(1, nh):
            for i in range(2):
                lower_copy(across(k), i).start()
        loads[0].wait()
        loads[2].wait()
        term = fwd[...] - is_last * bound[...]
        source[h] = term
        half = size // 2
        packed[h] = jnp.concatenate([term[:, :half], term[:, half:]], axis=0).astype(BF16)
        for k in range(1, nh):
            source_copy(across(k)).start()
        own_relay.start()

    @pl.when(t == 0)
    def _():
        for k in range(1, nh):
            diag_copy(across(k)).start()
        loads[0].wait()
        loads[2].wait()
        source[h] = fwd[...] - is_last * bound[...]

    send_diag = remote(diag_hbm.at[0], diag.at[mine], diag_sem.at[0], diag_sem.at[1], sibling)
    send_diag.start()

    high = fwd[...].astype(BF16)
    low = (fwd[...] - high.astype(F32)).astype(BF16)
    loads[1].wait()
    send_slab.wait()
    contract = (((1,), (1,)), ((), ()))
    part = lax.dot_general(high, slab[...], contract, preferred_element_type=F32)
    part = part + lax.dot_general(low, slab[...], contract, preferred_element_type=F32)
    loads[3].wait()
    parts[me] = (t == 0).astype(F32) * rhs[...] - part

    def part_copy(k):
        other = partner(k)
        return remote(
            parts.at[me], parts.at[me], parts_sems.at[0, other], parts_sems.at[1, me], coords(other)
        )

    for_each(1, nt * nh, lambda k: part_copy(k).start())

    highest = lax.Precision.HIGHEST
    loads[4].wait()
    gram = lax.dot_general(
        inv[...], inv[...], (((0,), (0,)), ((), ())), precision=highest, preferred_element_type=F32
    )

    def part_arrived(k):
        other = partner(k)
        remote(
            parts.at[other],
            parts.at[other],
            parts_sems.at[0, other],
            parts_sems.at[1, other],
            coords(other),
        ).wait_recv()

    for_each(1, nt * nh, part_arrived)
    total = parts[0:nh]
    for i in range(1, nt):
        total = total + parts[i * nh : (i + 1) * nh]
    answer = dot(total.reshape(nh * rows, fixed), gram, precision=highest)
    arrow_out[...] = answer.reshape(nh, rows, fixed)
    write_arrow = pltpu.make_async_copy(arrow_out.at[h], arrow_hbm, local_sem.at[8])
    write_arrow.start()
    answer = answer.astype(BF16)

    def relay(slot, j, i):
        return remote(slot, slot, relay_sems.at[0, j, i], relay_sems.at[1, j, i], sibling)

    def lower_piece(j, side, i):
        return lower.at[2 * j + side, piece_of(i)]

    def relay_on(slot, j, i):
        remote(slot, slot, lower_sems.at[0, j, i], lower_sems.at[1, j, i], {"tile": j}).wait_recv()
        relay(slot, j, i).start()

    def diag_arrived():
        loads[5].wait()
        slot = diag.at[2 * h + 1 - core]
        remote(slot, slot, diag_sem.at[0], diag_sem.at[1], sibling).wait_recv()

    def lower_arrived():
        load_lower.wait()
        relay(lower.at[2 * h + 1 - core], h, 0).wait_recv()
        for k in range(1, nh):
            j = across(k)
            for i in range(2):
                relay(lower_piece(j, 1 - core, i), j, i).wait_recv()

    def pair_of(q):
        return slice(2 * q, 2 * q + 2)

    def chain_copy(q, j):
        return remote(
            outgoing.at[pair_of(q)],
            incoming.at[h, pair_of(q)],
            chain_sems.at[0, j, q],
            chain_sems.at[1, h, q],
            {"tm": lax.rem(t + nt - 1, nt), "tile": j},
        )

    def row_copy(q, j):
        return remote(
            row_outgoing.at[q, j],
            row_incoming.at[h, q],
            row_sems.at[0, j, q],
            row_sems.at[1, h, q],
            {"tm": lax.rem(t + nt - 1, nt), "tile": j},
        )

    def out_copy(j):
        return remote(
            finished.at[j],
            sol_hbm.at[0, :, tile_rows(h)],
            out_sems.at[0, j],
            out_sems.at[1, h],
            {"tile": j},
        )

    @pl.when(t > 0)
    def _():
        for k in range(1, nh):
            j = across(k)
            remote(
                packed.at[j], packed.at[j], source_sems.at[0, j], source_sems.at[1, j], {"tile": j}
            ).wait_recv()
            term = packed[j].astype(F32)
            source[j] = jnp.concatenate([term[:rows], term[rows:]], axis=1)
        for c in range(chunks):
            columns = slice(c * width, (c + 1) * width)
            resid[c] = source[:, :, columns].reshape(nh * rows, width) - dot(
                answer, slab[:, columns]
            )
        accum[...] = jnp.zeros_like(accum)
        for k in range(1, nh):
            j = across(k)
            for i in range(2):
                relay_on(lower_piece(j, core, i), j, i)
        diag_arrived()
        pl.when(t < nt - 1)(lower_arrived)
        for q in reversed(range(nh)):

            @pl.when(h <= q)
            def _():
                @pl.when(t < nt - 1)
                def _():
                    for j in range(nh):
                        slot = incoming.at[j, pair_of(q)]
                        remote(
                            slot,
                            slot,
                            chain_sems.at[0, j, q],
                            chain_sems.at[1, j, q],
                            {"tm": lax.rem(t + 1, nt)},
                        ).wait_recv()
                    carry = incoming[0, pair_of(q)].astype(F32)
                    for j in range(1, nh):
                        carry = carry + incoming[j, pair_of(q)].astype(F32)
                    resid[pair_of(q)] = resid[pair_of(q)] - carry

                for b in range(2):
                    total = accum[b]
                    for c in (2 * q + 1, 2 * q):
                        weights = diag[2 * h + b, c * width : (c + 1) * width, :]
                        total = total + dot(resid[c].astype(BF16), weights)
                    accum[b] = total

        pl.when(t == nt - 1)(lower_arrived)
        first, second = accum[0].astype(BF16), accum[1].astype(BF16)

        def product(c):
            return dot(first, lower[c, 0:width, :]) + dot(second, lower[c, width:wide, :])

        @pl.when(t > 1)
        def _():
            for q in reversed(range(nh)):
                for c in (2 * q + 1, 2 * q):
                    outgoing[c] = product(c).astype(BF16)
                for j in range(q + 1):
                    chain_copy(q, j).start()

        @pl.when(t == 1)
        def _():
            for q in reversed(range(nh)):
                left, right = product(2 * q), product(2 * q + 1)
                for j in range(nh):
                    mix = slice(j * rows, (j + 1) * rows)
                    both = jnp.concatenate([left[mix], right[mix]], axis=0)
                    row_outgoing[q, j] = both.astype(BF16)
                    row_copy(q, j).start()

        for b in range(2):
            finished[:, :, b * width : (b + 1) * width] = accum[b].reshape(nh, rows, width)
        for k in range(1, nh):
            out_copy(across(k)).start()
        write_own = pltpu.make_async_copy(
            finished.at[h], sol_hbm.at[0, :, tile_rows(h)], local_sem.at[7]
        )
        write_own.start()

        for k in range(1, nh):
            j = across(k)
            source_copy(j).wait_send()
            for i in range(2):
                lower_copy(j, i).wait_send()
                relay(lower_piece(j, core, i), j, i).wait_send()
            out_copy(j).wait_send()
        own_relay.wait_send()

        @pl.when(t > 1)
        def _():
            for q in range(nh):
                for j in range(q + 1):
                    chain_copy(q, j).wait_send()

        @pl.when(t == 1)
        def _():
            for q in range(nh):
                for j in range(nh):
                    row_copy(q, j).wait_send()

        write_own.wait()
        for k in range(1, nh):
            j = across(k)
            slot = sol_hbm.at[0, :, tile_rows(j)]
            remote(slot, slot, out_sems.at[0, j], out_sems.at[1, j], {"tile": j}).wait_recv()

    @pl.when(t == 0)
    def _():
        own_answer = arrow_out[h].astype(BF16)
        for c in range(chunks):
            columns = slice(c * width, (c + 1) * width)
            resid[c, 0:rows, :] = source[h, :, columns] - dot(own_answer, slab[:, columns])
        row_accum[...] = jnp.zeros_like(row_accum)
        for k in range(1, nh):
            j = across(k)
            relay_on(diag.at[2 * j + core], j, 0)
        diag_arrived()
        for k in range(1, nh):
            j = across(k)
            relay(diag.at[2 * j + 1 - core], j, 0).wait_recv()
        for q in reversed(range(nh)):
            if nt > 1:
                carry = None
                for j in range(nh):
                    slot = row_incoming.at[j, q]
                    remote(
                        slot,
                        slot,
                        row_sems.at[0, j, q],
                        row_sems.at[1, j, q],
                        {"tm": lax.rem(t + 1, nt)},
                    ).wait_recv()
                    term = row_incoming[j, q].astype(F32)
                    carry = term if carry is None else carry + term
            for c in (2 * q + 1, 2 * q):
                value = resid[c, 0:rows, :]
                if nt > 1:
                    at = (c - 2 * q) * rows
                    value = value - carry[at : at + rows]
                rounded = value.astype(BF16)
                for b in range(c + 1):
                    row_accum[:, b * width : (b + 1) * width] += dot(
                        rounded, diag[b, c * width : (c + 1) * width, :]
                    )
        write_rows = pltpu.make_async_copy(row_accum, sol_hbm.at[0], local_sem.at[7])
        write_rows.start()
        for k in range(1, nh):
            j = across(k)
            diag_copy(j).wait_send()
            relay(diag.at[2 * j + core], j, 0).wait_send()
        write_rows.wait()

    for_each(1, nt * nh, lambda k: part_copy(k).wait_send())
    send_diag.wait_send()
    write_arrow.wait()


def solution(mesh):
    nt, nh = mesh.shape["tm"], mesh.shape["tile"]

    def shards(forward, rhs, diag, lower, slab, inverse, boundary):
        _, rows, size = forward.shape
        width = diag.shape[2]
        fixed = rhs.shape[1]
        chunks = 2 * nh
        everything = pl.BlockSpec(memory_space=pl.ANY)
        dma = pltpu.SemaphoreType.DMA
        return pl.pallas_call(
            functools.partial(kernel, nt, nh),
            out_shape=(
                jax.ShapeDtypeStruct(forward.shape, F32),
                jax.ShapeDtypeStruct(rhs.shape, F32),
            ),
            in_specs=[everything] * 7,
            out_specs=(everything, everything),
            scratch_shapes=[
                pltpu.VMEM((rows, size), F32),
                pltpu.VMEM((rows, fixed), F32),
                pltpu.VMEM((fixed, fixed), F32),
                pltpu.VMEM((rows, size), F32),
                pltpu.VMEM((fixed, size), BF16),
                pltpu.VMEM((chunks, size, width), BF16),
                pltpu.VMEM((chunks, 2 * width, width), BF16),
                pltpu.VMEM((nh, rows, size), F32),
                pltpu.VMEM((nh, 2 * rows, size // 2), BF16),
                pltpu.VMEM((nt * nh, rows, fixed), F32),
                pltpu.VMEM((chunks, nh * rows, width), F32),
                pltpu.VMEM((2, nh * rows, width), F32),
                pltpu.VMEM((chunks, nh * rows, width), BF16),
                pltpu.VMEM((nh, chunks, nh * rows, width), BF16),
                pltpu.VMEM((nh, nh, 2 * rows, width), BF16),
                pltpu.VMEM((nh, nh, 2 * rows, width), BF16),
                pltpu.VMEM((rows, size), F32),
                pltpu.VMEM((nh, rows, 2 * width), F32),
                pltpu.VMEM((nh, rows, fixed), F32),
                dma((9,)),
                dma((2,)),
                dma((2,)),
                dma((2, nh)),
                dma((2, nh, 2)),
                dma((2, nh, 2)),
                dma((2, nt * nh)),
                dma((2, nh, nh)),
                dma((2, nh)),
                dma((2, nh, nh)),
            ],
            compiler_params=pltpu.CompilerParams(
                collective_id=0, has_side_effects=True, vmem_limit_bytes=60 * 1024 * 1024
            ),
        )(forward, rhs, diag, lower, slab, inverse, boundary)

    return jax.shard_map(
        shards,
        mesh=mesh,
        in_specs=(
            P(("groups", "tm"), ("tile", "arrow"), None),
            P(("groups", "tile", "arrow"), None),
            P(("groups", "tm"), None, ("tile", "arrow")),
            P(("groups", "tm"), None, ("tile", "arrow")),
            P(("groups", "tm"), "arrow", None),
            P("groups", None),
            P(("groups", "tile", "arrow"), None),
        ),
        out_specs=(
            P(("groups", "tm"), ("tile", "arrow"), None),
            P(("groups", "tile", "arrow"), None),
        ),
        check_vma=False,
    )
```

```python
import functools

import jax
import jax.numpy as jnp
from jax import lax
from jax.experimental import pallas as pl
from jax.experimental.pallas import tpu as pltpu
from jax.sharding import PartitionSpec as P

MESH = pl.DeviceIdType.MESH
BF16 = jnp.bfloat16
F32 = jnp.float32
UNROLL_LIMIT = 8


def for_each(first, last, body):
    if last - first <= UNROLL_LIMIT:
        for i in range(first, last):
            body(i)
    else:
        pl.loop(first, last)(body)


def dot(a, b, **kwargs):
    return jnp.dot(a, b, preferred_element_type=F32, **kwargs)


def kernel(
    nt,
    nh,
    fwd_hbm,
    rhs_hbm,
    diag_hbm,
    lower_hbm,
    slab_hbm,
    inv_hbm,
    bound_hbm,
    sol_hbm,
    arrow_hbm,
    fwd,
    rhs,
    inv,
    bound,
    slab,
    diag,
    lower,
    source,
    packed,
    parts,
    resid,
    accum,
    outgoing,
    incoming,
    row_outgoing,
    row_incoming,
    row_accum,
    finished,
    arrow_out,
    local_sem,
    slab_sem,
    diag_sem,
    source_sems,
    lower_sems,
    relay_sems,
    parts_sems,
    chain_sems,
    out_sems,
    row_sems,
):
    t = lax.axis_index("tm")
    h = lax.axis_index("tile")
    core = lax.axis_index("arrow")
    sibling = {"arrow": 1 - core}
    rows = fwd.shape[0]
    size = diag.shape[1]
    width = diag.shape[2]
    wide = 2 * width
    chunks = 2 * nh
    halves = slab.shape[0] // 2
    fixed = slab.shape[0]
    me = t * nh + h
    own_rows = pl.ds(pl.multiple_of(core * halves, halves), halves)

    def tile_rows(j):
        return pl.ds(pl.multiple_of(j * wide, wide), wide)

    def remote(src, dst, send, recv, device):
        return pltpu.make_async_remote_copy(
            src_ref=src,
            dst_ref=dst,
            send_sem=send,
            recv_sem=recv,
            device_id=device,
            device_id_type=MESH,
        )

    def local(src, dst, index):
        return pltpu.make_async_copy(src, dst, local_sem.at[index])

    loads = [
        local(fwd_hbm.at[0], fwd, 0),
        local(slab_hbm.at[0], slab.at[own_rows], 1),
        local(bound_hbm, bound, 2),
        local(rhs_hbm, rhs, 3),
        local(inv_hbm, inv, 4),
        local(diag_hbm.at[0], diag.at[2 * h + core], 5),
    ]
    for load in loads:
        load.start()
    load_lower = local(lower_hbm.at[0, tile_rows(h)], lower.at[2 * h + core], 6)
    pl.when(t > 0)(load_lower.start)

    def coords(index):
        return {"tm": index // nh, "tile": lax.rem(index, nh)}

    def partner(k):
        return lax.rem(me + k, nt * nh)

    def across(k):
        return lax.rem(h + k, nh)

    barrier = pltpu.get_barrier_semaphore()
    pl.semaphore_signal(barrier, inc=1, device_id=sibling, device_id_type=MESH)

    def greet(k):
        pl.semaphore_signal(barrier, inc=1, device_id=coords(partner(k)), device_id_type=MESH)

    for_each(1, nt * nh, greet)
    pl.semaphore_wait(barrier, nt * nh)

    send_slab = remote(
        slab_hbm.at[0], slab.at[own_rows], slab_sem.at[0], slab_sem.at[1], sibling
    )
    send_slab.start()

    is_last = (t == nt - 1).astype(F32)
    mine = 2 * h + core

    def source_copy(j):
        return remote(
            packed.at[h], packed.at[h], source_sems.at[0, j], source_sems.at[1, h], {"tile": j}
        )

    def piece_of(i):
        return slice(i * width, (i + 1) * width)

    def lower_copy(j, i):
        return remote(
            lower_hbm.at[0, pl.ds(pl.multiple_of(j * wide + i * width, width), width)],
            lower.at[mine, piece_of(i)],
            lower_sems.at[0, j, i],
            lower_sems.at[1, h, i],
            {"tile": j},
        )

    def diag_copy(j):
        return remote(
            diag_hbm.at[0],
            diag.at[mine],
            lower_sems.at[0, j, 0],
            lower_sems.at[1, h, 0],
            {"tile": j},
        )

    own_relay = remote(
        lower_hbm.at[0, tile_rows(h)],
        lower.at[mine],
        relay_sems.at[0, h, 0],
        relay_sems.at[1, h, 0],
        sibling,
    )

    @pl.when(t > 0)
    def _():
        for k in range(1, nh):
            for i in range(2):
                lower_copy(across(k), i).start()
        loads[0].wait()
        loads[2].wait()
        term = fwd[...] - is_last * bound[...]
        source[h] = term
        half = size // 2
        packed[h] = jnp.concatenate([term[:, :half], term[:, half:]], axis=0).astype(BF16)
        for k in range(1, nh):
            source_copy(across(k)).start()
        own_relay.start()

    @pl.when(t == 0)
    def _():
        for k in range(1, nh):
            diag_copy(across(k)).start()
        loads[0].wait()
        loads[2].wait()
        source[h] = fwd[...] - is_last * bound[...]

    send_diag = remote(diag_hbm.at[0], diag.at[mine], diag_sem.at[0], diag_sem.at[1], sibling)
    send_diag.start()

    high = fwd[...].astype(BF16)
    low = (fwd[...] - high.astype(F32)).astype(BF16)
    loads[1].wait()
    send_slab.wait()
    contract = (((1,), (1,)), ((), ()))
    part = lax.dot_general(high, slab[...], contract, preferred_element_type=F32)
    part = part + lax.dot_general(low, slab[...], contract, preferred_element_type=F32)
    loads[3].wait()
    parts[me] = (t == 0).astype(F32) * rhs[...] - part

    def part_copy(k):
        other = partner(k)
        return remote(
            parts.at[me], parts.at[me], parts_sems.at[0, other], parts_sems.at[1, me], coords(other)
        )

    for_each(1, nt * nh, lambda k: part_copy(k).start())

    highest = lax.Precision.HIGHEST
    loads[4].wait()
    gram = lax.dot_general(
        inv[...], inv[...], (((0,), (0,)), ((), ())), precision=highest, preferred_element_type=F32
    )

    def part_arrived(k):
        other = partner(k)
        remote(
            parts.at[other],
            parts.at[other],
            parts_sems.at[0, other],
            parts_sems.at[1, other],
            coords(other),
        ).wait_recv()

    for_each(1, nt * nh, part_arrived)
    total = parts[0:nh]
    for i in range(1, nt):
        total = total + parts[i * nh : (i + 1) * nh]
    answer = dot(total.reshape(nh * rows, fixed), gram, precision=highest)
    arrow_out[...] = answer.reshape(nh, rows, fixed)
    write_arrow = pltpu.make_async_copy(arrow_out.at[h], arrow_hbm, local_sem.at[8])
    write_arrow.start()
    answer = answer.astype(BF16)

    def relay(slot, j, i):
        return remote(slot, slot, relay_sems.at[0, j, i], relay_sems.at[1, j, i], sibling)

    def lower_piece(j, side, i):
        return lower.at[2 * j + side, piece_of(i)]

    def relay_on(slot, j, i):
        remote(slot, slot, lower_sems.at[0, j, i], lower_sems.at[1, j, i], {"tile": j}).wait_recv()
        relay(slot, j, i).start()

    def diag_arrived():
        loads[5].wait()
        slot = diag.at[2 * h + 1 - core]
        remote(slot, slot, diag_sem.at[0], diag_sem.at[1], sibling).wait_recv()

    def lower_arrived():
        load_lower.wait()
        relay(lower.at[2 * h + 1 - core], h, 0).wait_recv()
        for k in range(1, nh):
            j = across(k)
            for i in range(2):
                relay(lower_piece(j, 1 - core, i), j, i).wait_recv()

    def pair_of(q):
        return slice(2 * q, 2 * q + 2)

    def chain_copy(q, j):
        return remote(
            outgoing.at[pair_of(q)],
            incoming.at[h, pair_of(q)],
            chain_sems.at[0, j, q],
            chain_sems.at[1, h, q],
            {"tm": lax.rem(t + nt - 1, nt), "tile": j},
        )

    def row_copy(q, j):
        return remote(
            row_outgoing.at[q, j],
            row_incoming.at[h, q],
            row_sems.at[0, j, q],
            row_sems.at[1, h, q],
            {"tm": lax.rem(t + nt - 1, nt), "tile": j},
        )

    def out_copy(j):
        return remote(
            finished.at[j],
            sol_hbm.at[0, :, tile_rows(h)],
            out_sems.at[0, j],
            out_sems.at[1, h],
            {"tile": j},
        )

    @pl.when(t > 0)
    def _():
        for k in range(1, nh):
            j = across(k)
            for i in range(2):
                relay_on(lower_piece(j, core, i), j, i)
        for k in range(1, nh):
            j = across(k)
            remote(
                packed.at[j], packed.at[j], source_sems.at[0, j], source_sems.at[1, j], {"tile": j}
            ).wait_recv()
            term = packed[j].astype(F32)
            source[j] = jnp.concatenate([term[:rows], term[rows:]], axis=1)
        for c in range(chunks):
            columns = slice(c * width, (c + 1) * width)
            resid[c] = source[:, :, columns].reshape(nh * rows, width) - dot(
                answer, slab[:, columns]
            )
        accum[...] = jnp.zeros_like(accum)
        diag_arrived()
        pl.when(t < nt - 1)(lower_arrived)
        for q in reversed(range(nh)):

            @pl.when(h <= q)
            def _():
                @pl.when(t < nt - 1)
                def _():
                    for j in range(nh):
                        slot = incoming.at[j, pair_of(q)]
                        remote(
                            slot,
                            slot,
                            chain_sems.at[0, j, q],
                            chain_sems.at[1, j, q],
                            {"tm": lax.rem(t + 1, nt)},
                        ).wait_recv()
                    carry = incoming[0, pair_of(q)].astype(F32)
                    for j in range(1, nh):
                        carry = carry + incoming[j, pair_of(q)].astype(F32)
                    resid[pair_of(q)] = resid[pair_of(q)] - carry

                for b in range(2):
                    total = accum[b]
                    for c in (2 * q + 1, 2 * q):
                        weights = diag[2 * h + b, c * width : (c + 1) * width, :]
                        total = total + dot(resid[c].astype(BF16), weights)
                    accum[b] = total

        pl.when(t == nt - 1)(lower_arrived)
        first, second = accum[0].astype(BF16), accum[1].astype(BF16)

        def product(c):
            return dot(first, lower[c, 0:width, :]) + dot(second, lower[c, width:wide, :])

        @pl.when(t > 1)
        def _():
            for q in reversed(range(nh)):
                for c in (2 * q + 1, 2 * q):
                    outgoing[c] = product(c).astype(BF16)
                for j in range(q + 1):
                    chain_copy(q, j).start()

        @pl.when(t == 1)
        def _():
            for q in reversed(range(nh)):
                left, right = product(2 * q), product(2 * q + 1)
                for j in range(nh):
                    mix = slice(j * rows, (j + 1) * rows)
                    both = jnp.concatenate([left[mix], right[mix]], axis=0)
                    row_outgoing[q, j] = both.astype(BF16)
                    row_copy(q, j).start()

        for b in range(2):
            finished[:, :, b * width : (b + 1) * width] = accum[b].reshape(nh, rows, width)
        for k in range(1, nh):
            out_copy(across(k)).start()
        write_own = pltpu.make_async_copy(
            finished.at[h], sol_hbm.at[0, :, tile_rows(h)], local_sem.at[7]
        )
        write_own.start()

        for k in range(1, nh):
            j = across(k)
            source_copy(j).wait_send()
            for i in range(2):
                lower_copy(j, i).wait_send()
                relay(lower_piece(j, core, i), j, i).wait_send()
            out_copy(j).wait_send()
        own_relay.wait_send()

        @pl.when(t > 1)
        def _():
            for q in range(nh):
                for j in range(q + 1):
                    chain_copy(q, j).wait_send()

        @pl.when(t == 1)
        def _():
            for q in range(nh):
                for j in range(nh):
                    row_copy(q, j).wait_send()

        write_own.wait()
        for k in range(1, nh):
            j = across(k)
            slot = sol_hbm.at[0, :, tile_rows(j)]
            remote(slot, slot, out_sems.at[0, j], out_sems.at[1, j], {"tile": j}).wait_recv()

    @pl.when(t == 0)
    def _():
        own_answer = arrow_out[h].astype(BF16)
        for c in range(chunks):
            columns = slice(c * width, (c + 1) * width)
            resid[c, 0:rows, :] = source[h, :, columns] - dot(own_answer, slab[:, columns])
        row_accum[...] = jnp.zeros_like(row_accum)
        for k in range(1, nh):
            j = across(k)
            relay_on(diag.at[2 * j + core], j, 0)
        diag_arrived()
        for k in range(1, nh):
            j = across(k)
            relay(diag.at[2 * j + 1 - core], j, 0).wait_recv()
        for q in reversed(range(nh)):
            if nt > 1:
                carry = None
                for j in range(nh):
                    slot = row_incoming.at[j, q]
                    remote(
                        slot,
                        slot,
                        row_sems.at[0, j, q],
                        row_sems.at[1, j, q],
                        {"tm": lax.rem(t + 1, nt)},
                    ).wait_recv()
                    term = row_incoming[j, q].astype(F32)
                    carry = term if carry is None else carry + term
            for c in (2 * q + 1, 2 * q):
                value = resid[c, 0:rows, :]
                if nt > 1:
                    at = (c - 2 * q) * rows
                    value = value - carry[at : at + rows]
                rounded = value.astype(BF16)
                for b in range(c + 1):
                    row_accum[:, b * width : (b + 1) * width] += dot(
                        rounded, diag[b, c * width : (c + 1) * width, :]
                    )
        write_rows = pltpu.make_async_copy(row_accum, sol_hbm.at[0], local_sem.at[7])
        write_rows.start()
        for k in range(1, nh):
            j = across(k)
            diag_copy(j).wait_send()
            relay(diag.at[2 * j + core], j, 0).wait_send()
        write_rows.wait()

    for_each(1, nt * nh, lambda k: part_copy(k).wait_send())
    send_diag.wait_send()
    write_arrow.wait()


def solution(mesh):
    nt, nh = mesh.shape["tm"], mesh.shape["tile"]

    def shards(forward, rhs, diag, lower, slab, inverse, boundary):
        _, rows, size = forward.shape
        width = diag.shape[2]
        fixed = rhs.shape[1]
        chunks = 2 * nh
        everything = pl.BlockSpec(memory_space=pl.ANY)
        dma = pltpu.SemaphoreType.DMA
        return pl.pallas_call(
            functools.partial(kernel, nt, nh),
            out_shape=(
                jax.ShapeDtypeStruct(forward.shape, F32),
                jax.ShapeDtypeStruct(rhs.shape, F32),
            ),
            in_specs=[everything] * 7,
            out_specs=(everything, everything),
            scratch_shapes=[
                pltpu.VMEM((rows, size), F32),
                pltpu.VMEM((rows, fixed), F32),
                pltpu.VMEM((fixed, fixed), F32),
                pltpu.VMEM((rows, size), F32),
                pltpu.VMEM((fixed, size), BF16),
                pltpu.VMEM((chunks, size, width), BF16),
                pltpu.VMEM((chunks, 2 * width, width), BF16),
                pltpu.VMEM((nh, rows, size), F32),
                pltpu.VMEM((nh, 2 * rows, size // 2), BF16),
                pltpu.VMEM((nt * nh, rows, fixed), F32),
                pltpu.VMEM((chunks, nh * rows, width), F32),
                pltpu.VMEM((2, nh * rows, width), F32),
                pltpu.VMEM((chunks, nh * rows, width), BF16),
                pltpu.VMEM((nh, chunks, nh * rows, width), BF16),
                pltpu.VMEM((nh, nh, 2 * rows, width), BF16),
                pltpu.VMEM((nh, nh, 2 * rows, width), BF16),
                pltpu.VMEM((rows, size), F32),
                pltpu.VMEM((nh, rows, 2 * width), F32),
                pltpu.VMEM((nh, rows, fixed), F32),
                dma((9,)),
                dma((2,)),
                dma((2,)),
                dma((2, nh)),
                dma((2, nh, 2)),
                dma((2, nh, 2)),
                dma((2, nt * nh)),
                dma((2, nh, nh)),
                dma((2, nh)),
                dma((2, nh, nh)),
            ],
            compiler_params=pltpu.CompilerParams(
                collective_id=0, has_side_effects=True, vmem_limit_bytes=60 * 1024 * 1024
            ),
        )(forward, rhs, diag, lower, slab, inverse, boundary)

    return jax.shard_map(
        shards,
        mesh=mesh,
        in_specs=(
            P(("groups", "tm"), ("tile", "arrow"), None),
            P(("groups", "tile", "arrow"), None),
            P(("groups", "tm"), None, ("tile", "arrow")),
            P(("groups", "tm"), None, ("tile", "arrow")),
            P(("groups", "tm"), "arrow", None),
            P("groups", None),
            P(("groups", "tile", "arrow"), None),
        ),
        out_specs=(
            P(("groups", "tm"), ("tile", "arrow"), None),
            P(("groups", "tile", "arrow"), None),
        ),
        check_vma=False,
    )
```

```python
import functools

import jax
import jax.numpy as jnp
from jax import lax
from jax.experimental import pallas as pl
from jax.experimental.pallas import tpu as pltpu
from jax.sharding import PartitionSpec as P

MESH = pl.DeviceIdType.MESH
BF16 = jnp.bfloat16
F32 = jnp.float32
UNROLL_LIMIT = 8


def for_each(first, last, body):
    if last - first <= UNROLL_LIMIT:
        for i in range(first, last):
            body(i)
    else:
        pl.loop(first, last)(body)


def dot(a, b, **kwargs):
    return jnp.dot(a, b, preferred_element_type=F32, **kwargs)


def kernel(
    nt,
    nh,
    fwd_hbm,
    rhs_hbm,
    diag_hbm,
    lower_hbm,
    slab_hbm,
    inv_hbm,
    bound_hbm,
    sol_hbm,
    arrow_hbm,
    fwd,
    rhs,
    inv,
    bound,
    slab,
    diag,
    lower,
    source,
    packed,
    parts,
    resid,
    accum,
    outgoing,
    incoming,
    row_outgoing,
    row_incoming,
    row_accum,
    finished,
    arrow_out,
    local_sem,
    slab_sem,
    diag_sem,
    source_sems,
    lower_sems,
    relay_sems,
    parts_sems,
    chain_sems,
    out_sems,
    row_sems,
):
    t = lax.axis_index("tm")
    h = lax.axis_index("tile")
    core = lax.axis_index("arrow")
    sibling = {"arrow": 1 - core}
    rows = fwd.shape[0]
    size = diag.shape[1]
    width = diag.shape[2]
    wide = 2 * width
    chunks = 2 * nh
    halves = slab.shape[0] // 2
    fixed = slab.shape[0]
    me = t * nh + h
    own_rows = pl.ds(pl.multiple_of(core * halves, halves), halves)

    def tile_rows(j):
        return pl.ds(pl.multiple_of(j * wide, wide), wide)

    def remote(src, dst, send, recv, device):
        return pltpu.make_async_remote_copy(
            src_ref=src,
            dst_ref=dst,
            send_sem=send,
            recv_sem=recv,
            device_id=device,
            device_id_type=MESH,
        )

    def local(src, dst, index):
        return pltpu.make_async_copy(src, dst, local_sem.at[index])

    loads = [
        local(fwd_hbm.at[0], fwd, 0),
        local(slab_hbm.at[0], slab.at[own_rows], 1),
        local(bound_hbm, bound, 2),
        local(rhs_hbm, rhs, 3),
        local(inv_hbm, inv, 4),
        local(diag_hbm.at[0], diag.at[2 * h + core], 5),
    ]
    for load in loads:
        load.start()
    load_lower = local(lower_hbm.at[0, tile_rows(h)], lower.at[2 * h + core], 6)
    pl.when(t > 0)(load_lower.start)

    def coords(index):
        return {"tm": index // nh, "tile": lax.rem(index, nh)}

    def partner(k):
        return lax.rem(me + k, nt * nh)

    def across(k):
        return lax.rem(h + k, nh)

    barrier = pltpu.get_barrier_semaphore()
    pl.semaphore_signal(barrier, inc=1, device_id=sibling, device_id_type=MESH)

    def greet(k):
        pl.semaphore_signal(barrier, inc=1, device_id=coords(partner(k)), device_id_type=MESH)

    for_each(1, nt * nh, greet)
    pl.semaphore_wait(barrier, nt * nh)

    send_slab = remote(
        slab_hbm.at[0], slab.at[own_rows], slab_sem.at[0], slab_sem.at[1], sibling
    )
    send_slab.start()

    is_last = (t == nt - 1).astype(F32)
    mine = 2 * h + core

    def source_copy(j):
        return remote(
            packed.at[h], packed.at[h], source_sems.at[0, j], source_sems.at[1, h], {"tile": j}
        )

    def piece_of(i):
        return slice(i * width, (i + 1) * width)

    def lower_copy(j, i):
        return remote(
            lower_hbm.at[0, pl.ds(pl.multiple_of(j * wide + i * width, width), width)],
            lower.at[mine, piece_of(i)],
            lower_sems.at[0, j, i],
            lower_sems.at[1, h, i],
            {"tile": j},
        )

    def diag_copy(j):
        return remote(
            diag_hbm.at[0],
            diag.at[mine],
            lower_sems.at[0, j, 0],
            lower_sems.at[1, h, 0],
            {"tile": j},
        )

    own_relay = remote(
        lower_hbm.at[0, tile_rows(h)],
        lower.at[mine],
        relay_sems.at[0, h, 0],
        relay_sems.at[1, h, 0],
        sibling,
    )

    @pl.when(t > 0)
    def _():
        for k in range(1, nh):
            lower_copy(across(k), 0).start()
        loads[0].wait()
        loads[2].wait()
        term = fwd[...] - is_last * bound[...]
        source[h] = term
        half = size // 2
        packed[h] = jnp.concatenate([term[:, :half], term[:, half:]], axis=0).astype(BF16)
        for k in range(1, nh):
            source_copy(across(k)).start()
        for k in range(1, nh):
            lower_copy(across(k), 1).start()
        own_relay.start()

    @pl.when(t == 0)
    def _():
        for k in range(1, nh):
            diag_copy(across(k)).start()
        loads[0].wait()
        loads[2].wait()
        source[h] = fwd[...] - is_last * bound[...]

    send_diag = remote(diag_hbm.at[0], diag.at[mine], diag_sem.at[0], diag_sem.at[1], sibling)
    send_diag.start()

    high = fwd[...].astype(BF16)
    low = (fwd[...] - high.astype(F32)).astype(BF16)
    loads[1].wait()
    send_slab.wait()
    contract = (((1,), (1,)), ((), ()))
    part = lax.dot_general(high, slab[...], contract, preferred_element_type=F32)
    part = part + lax.dot_general(low, slab[...], contract, preferred_element_type=F32)
    loads[3].wait()
    parts[me] = (t == 0).astype(F32) * rhs[...] - part

    def part_copy(k):
        other = partner(k)
        return remote(
            parts.at[me], parts.at[me], parts_sems.at[0, other], parts_sems.at[1, me], coords(other)
        )

    for_each(1, nt * nh, lambda k: part_copy(k).start())

    highest = lax.Precision.HIGHEST
    loads[4].wait()
    gram = lax.dot_general(
        inv[...], inv[...], (((0,), (0,)), ((), ())), precision=highest, preferred_element_type=F32
    )

    def part_arrived(k):
        other = partner(k)
        remote(
            parts.at[other],
            parts.at[other],
            parts_sems.at[0, other],
            parts_sems.at[1, other],
            coords(other),
        ).wait_recv()

    for_each(1, nt * nh, part_arrived)
    total = parts[0:nh]
    for i in range(1, nt):
        total = total + parts[i * nh : (i + 1) * nh]
    answer = dot(total.reshape(nh * rows, fixed), gram, precision=highest)
    arrow_out[...] = answer.reshape(nh, rows, fixed)
    write_arrow = pltpu.make_async_copy(arrow_out.at[h], arrow_hbm, local_sem.at[8])
    write_arrow.start()
    answer = answer.astype(BF16)

    def relay(slot, j, i):
        return remote(slot, slot, relay_sems.at[0, j, i], relay_sems.at[1, j, i], sibling)

    def lower_piece(j, side, i):
        return lower.at[2 * j + side, piece_of(i)]

    def relay_on(slot, j, i):
        remote(slot, slot, lower_sems.at[0, j, i], lower_sems.at[1, j, i], {"tile": j}).wait_recv()
        relay(slot, j, i).start()

    def diag_arrived():
        loads[5].wait()
        slot = diag.at[2 * h + 1 - core]
        remote(slot, slot, diag_sem.at[0], diag_sem.at[1], sibling).wait_recv()

    def lower_arrived():
        load_lower.wait()
        relay(lower.at[2 * h + 1 - core], h, 0).wait_recv()
        for k in range(1, nh):
            j = across(k)
            for i in range(2):
                relay(lower_piece(j, 1 - core, i), j, i).wait_recv()

    def pair_of(q):
        return slice(2 * q, 2 * q + 2)

    def chain_copy(q, j):
        return remote(
            outgoing.at[pair_of(q)],
            incoming.at[h, pair_of(q)],
            chain_sems.at[0, j, q],
            chain_sems.at[1, h, q],
            {"tm": lax.rem(t + nt - 1, nt), "tile": j},
        )

    def row_copy(q, j):
        return remote(
            row_outgoing.at[q, j],
            row_incoming.at[h, q],
            row_sems.at[0, j, q],
            row_sems.at[1, h, q],
            {"tm": lax.rem(t + nt - 1, nt), "tile": j},
        )

    def out_copy(j):
        return remote(
            finished.at[j],
            sol_hbm.at[0, :, tile_rows(h)],
            out_sems.at[0, j],
            out_sems.at[1, h],
            {"tile": j},
        )

    @pl.when(t > 0)
    def _():
        for k in range(1, nh):
            j = across(k)
            for i in range(2):
                relay_on(lower_piece(j, core, i), j, i)
        for k in range(1, nh):
            j = across(k)
            remote(
                packed.at[j], packed.at[j], source_sems.at[0, j], source_sems.at[1, j], {"tile": j}
            ).wait_recv()
            term = packed[j].astype(F32)
            source[j] = jnp.concatenate([term[:rows], term[rows:]], axis=1)
        for c in range(chunks):
            columns = slice(c * width, (c + 1) * width)
            resid[c] = source[:, :, columns].reshape(nh * rows, width) - dot(
                answer, slab[:, columns]
            )
        accum[...] = jnp.zeros_like(accum)
        diag_arrived()
        pl.when(t < nt - 1)(lower_arrived)
        for q in reversed(range(nh)):

            @pl.when(h <= q)
            def _():
                @pl.when(t < nt - 1)
                def _():
                    for j in range(nh):
                        slot = incoming.at[j, pair_of(q)]
                        remote(
                            slot,
                            slot,
                            chain_sems.at[0, j, q],
                            chain_sems.at[1, j, q],
                            {"tm": lax.rem(t + 1, nt)},
                        ).wait_recv()
                    carry = incoming[0, pair_of(q)].astype(F32)
                    for j in range(1, nh):
                        carry = carry + incoming[j, pair_of(q)].astype(F32)
                    resid[pair_of(q)] = resid[pair_of(q)] - carry

                for b in range(2):
                    total = accum[b]
                    for c in (2 * q + 1, 2 * q):
                        weights = diag[2 * h + b, c * width : (c + 1) * width, :]
                        total = total + dot(resid[c].astype(BF16), weights)
                    accum[b] = total

        pl.when(t == nt - 1)(lower_arrived)
        first, second = accum[0].astype(BF16), accum[1].astype(BF16)

        def product(c):
            return dot(first, lower[c, 0:width, :]) + dot(second, lower[c, width:wide, :])

        @pl.when(t > 1)
        def _():
            for q in reversed(range(nh)):
                for c in (2 * q + 1, 2 * q):
                    outgoing[c] = product(c).astype(BF16)
                for j in range(q + 1):
                    chain_copy(q, j).start()

        @pl.when(t == 1)
        def _():
            for q in reversed(range(nh)):
                left, right = product(2 * q), product(2 * q + 1)
                for j in range(nh):
                    mix = slice(j * rows, (j + 1) * rows)
                    both = jnp.concatenate([left[mix], right[mix]], axis=0)
                    row_outgoing[q, j] = both.astype(BF16)
                    row_copy(q, j).start()

        for b in range(2):
            finished[:, :, b * width : (b + 1) * width] = accum[b].reshape(nh, rows, width)
        for k in range(1, nh):
            out_copy(across(k)).start()
        write_own = pltpu.make_async_copy(
            finished.at[h], sol_hbm.at[0, :, tile_rows(h)], local_sem.at[7]
        )
        write_own.start()

        for k in range(1, nh):
            j = across(k)
            source_copy(j).wait_send()
            for i in range(2):
                lower_copy(j, i).wait_send()
                relay(lower_piece(j, core, i), j, i).wait_send()
            out_copy(j).wait_send()
        own_relay.wait_send()

        @pl.when(t > 1)
        def _():
            for q in range(nh):
                for j in range(q + 1):
                    chain_copy(q, j).wait_send()

        @pl.when(t == 1)
        def _():
            for q in range(nh):
                for j in range(nh):
                    row_copy(q, j).wait_send()

        write_own.wait()
        for k in range(1, nh):
            j = across(k)
            slot = sol_hbm.at[0, :, tile_rows(j)]
            remote(slot, slot, out_sems.at[0, j], out_sems.at[1, j], {"tile": j}).wait_recv()

    @pl.when(t == 0)
    def _():
        own_answer = arrow_out[h].astype(BF16)
        for c in range(chunks):
            columns = slice(c * width, (c + 1) * width)
            resid[c, 0:rows, :] = source[h, :, columns] - dot(own_answer, slab[:, columns])
        row_accum[...] = jnp.zeros_like(row_accum)
        for k in range(1, nh):
            j = across(k)
            relay_on(diag.at[2 * j + core], j, 0)
        diag_arrived()
        for k in range(1, nh):
            j = across(k)
            relay(diag.at[2 * j + 1 - core], j, 0).wait_recv()
        for q in reversed(range(nh)):
            if nt > 1:
                carry = None
                for j in range(nh):
                    slot = row_incoming.at[j, q]
                    remote(
                        slot,
                        slot,
                        row_sems.at[0, j, q],
                        row_sems.at[1, j, q],
                        {"tm": lax.rem(t + 1, nt)},
                    ).wait_recv()
                    term = row_incoming[j, q].astype(F32)
                    carry = term if carry is None else carry + term
            for c in (2 * q + 1, 2 * q):
                value = resid[c, 0:rows, :]
                if nt > 1:
                    at = (c - 2 * q) * rows
                    value = value - carry[at : at + rows]
                rounded = value.astype(BF16)
                for b in range(c + 1):
                    row_accum[:, b * width : (b + 1) * width] += dot(
                        rounded, diag[b, c * width : (c + 1) * width, :]
                    )
        write_rows = pltpu.make_async_copy(row_accum, sol_hbm.at[0], local_sem.at[7])
        write_rows.start()
        for k in range(1, nh):
            j = across(k)
            diag_copy(j).wait_send()
            relay(diag.at[2 * j + core], j, 0).wait_send()
        write_rows.wait()

    for_each(1, nt * nh, lambda k: part_copy(k).wait_send())
    send_diag.wait_send()
    write_arrow.wait()


def solution(mesh):
    nt, nh = mesh.shape["tm"], mesh.shape["tile"]

    def shards(forward, rhs, diag, lower, slab, inverse, boundary):
        _, rows, size = forward.shape
        width = diag.shape[2]
        fixed = rhs.shape[1]
        chunks = 2 * nh
        everything = pl.BlockSpec(memory_space=pl.ANY)
        dma = pltpu.SemaphoreType.DMA
        return pl.pallas_call(
            functools.partial(kernel, nt, nh),
            out_shape=(
                jax.ShapeDtypeStruct(forward.shape, F32),
                jax.ShapeDtypeStruct(rhs.shape, F32),
            ),
            in_specs=[everything] * 7,
            out_specs=(everything, everything),
            scratch_shapes=[
                pltpu.VMEM((rows, size), F32),
                pltpu.VMEM((rows, fixed), F32),
                pltpu.VMEM((fixed, fixed), F32),
                pltpu.VMEM((rows, size), F32),
                pltpu.VMEM((fixed, size), BF16),
                pltpu.VMEM((chunks, size, width), BF16),
                pltpu.VMEM((chunks, 2 * width, width), BF16),
                pltpu.VMEM((nh, rows, size), F32),
                pltpu.VMEM((nh, 2 * rows, size // 2), BF16),
                pltpu.VMEM((nt * nh, rows, fixed), F32),
                pltpu.VMEM((chunks, nh * rows, width), F32),
                pltpu.VMEM((2, nh * rows, width), F32),
                pltpu.VMEM((chunks, nh * rows, width), BF16),
                pltpu.VMEM((nh, chunks, nh * rows, width), BF16),
                pltpu.VMEM((nh, nh, 2 * rows, width), BF16),
                pltpu.VMEM((nh, nh, 2 * rows, width), BF16),
                pltpu.VMEM((rows, size), F32),
                pltpu.VMEM((nh, rows, 2 * width), F32),
                pltpu.VMEM((nh, rows, fixed), F32),
                dma((9,)),
                dma((2,)),
                dma((2,)),
                dma((2, nh)),
                dma((2, nh, 2)),
                dma((2, nh, 2)),
                dma((2, nt * nh)),
                dma((2, nh, nh)),
                dma((2, nh)),
                dma((2, nh, nh)),
            ],
            compiler_params=pltpu.CompilerParams(
                collective_id=0, has_side_effects=True, vmem_limit_bytes=60 * 1024 * 1024
            ),
        )(forward, rhs, diag, lower, slab, inverse, boundary)

    return jax.shard_map(
        shards,
        mesh=mesh,
        in_specs=(
            P(("groups", "tm"), ("tile", "arrow"), None),
            P(("groups", "tile", "arrow"), None),
            P(("groups", "tm"), None, ("tile", "arrow")),
            P(("groups", "tm"), None, ("tile", "arrow")),
            P(("groups", "tm"), "arrow", None),
            P("groups", None),
            P(("groups", "tile", "arrow"), None),
        ),
        out_specs=(
            P(("groups", "tm"), ("tile", "arrow"), None),
            P(("groups", "tile", "arrow"), None),
        ),
        check_vma=False,
    )
```
